32 devices in a mesh: shot: 4 (over y, core), slab: 8 (over z, x).
Axes of the slice: x: 2, y: 2, z: 4, core: 2. Of those that a mesh axis runs over, the one named last changes fastest.
Arguments:
- source_field: bfloat16 [12, 8, 32, 256, 128], P('shot', None, 'slab'), may hold values from -4 to 4
- receiver_field: bfloat16 [12, 8, 32, 256, 128], P('shot', None, 'slab'), may hold values from -4 to 4
- shot_group: int32 [12], replicated, may hold values from 0 to 11
- first_weight: bfloat16 [32, 12, 3, 3, 3], replicated, may hold values from -0.3125 to 0.3125
- first_bias: float32 [32], replicated, may hold values from -3 to 3
- second_weight: bfloat16 [32, 32, 3, 3, 3], replicated, may hold values from -0.21875 to 0.21875
- second_bias: float32 [32], replicated, may hold values from -3 to 3
Outputs:
- features: bfloat16 [32, 32, 256, 128], P(None, 'shot', 'slab')
The draws below stay inside these ranges and needn't reach their ends.
All inputs are finite; a program needn't handle non-finite values.
Results may differ from the reference program's by a relative error of at most 0.01.
Values may be sent and summed in bfloat16 or wider, within the bound.
A program may use at most 128 MiB of HBM per device.

```python
import math
import jax
import jax.numpy as jnp
from jax import lax

GROUPS = 12
CH = 32
TSTEPS = 8
NX = 256
NY = 128
SHOTS = 12
NZ = 32


def touch_ends(drawn, rng, smallest, high):
    spot = [jax.random.randint(jax.random.fold_in(rng, axis), (), 0, length) for axis, length in enumerate(drawn.shape)]
    longest = drawn.shape.index(max(drawn.shape))
    neighbour = spot[:longest] + [(spot[longest] + 1) % drawn.shape[longest]] + spot[longest + 1:]
    return drawn.at[tuple(spot)].set(smallest).at[tuple(neighbour)].set(high)


def steps_of(rng, shape, split, least, high):
    loudness = 1.0
    for dim, shards_of in split:
        steps = jax.random.uniform(jax.random.fold_in(jax.random.fold_in(rng, 6), dim), (shards_of,), jnp.float32, least / len(split), high / len(split))
        loudness = loudness * jnp.repeat(jnp.exp(steps), shape[dim] // shards_of).reshape((-1,) + (1,) * (len(shape) - 1 - dim))
    return loudness


def normal_values(stream_key, extent, scale, limit, shards=(), kind=jnp.bfloat16):
    values = scale * jax.random.normal(stream_key, extent, jnp.float32)
    if shards:
        values = values * steps_of(stream_key, extent, shards, -0.22, 0.18)
    return jnp.clip(values, -limit, limit).astype(kind)


def setup_inputs(seed: int = 0) -> dict:
    seeds = jax.random.split(jax.random.key(seed), 8)
    return {
        "source_field": normal_values(seeds[0], (SHOTS, TSTEPS, NZ, NX, NY), 0.6, 4.0, ((0, 4), (2, 8))),
        "receiver_field": normal_values(seeds[1], (SHOTS, TSTEPS, NZ, NX, NY), 0.6, 4.0, ((0, 4), (2, 8))),
        "shot_group": touch_ends(jax.random.randint(seeds[2], (SHOTS,), 0, GROUPS), jax.random.fold_in(seeds[2], 1), 0, GROUPS - 1).astype(jnp.int32),
        "first_weight": normal_values(seeds[3], (CH, GROUPS, 3, 3, 3), (GROUPS * 27) ** -0.5, 0.3125),
        "first_bias": normal_values(seeds[4], (CH,), 0.5, 3.0, (), jnp.float32),
        "second_weight": normal_values(seeds[5], (CH, CH, 3, 3, 3), (CH * 27) ** -0.5, 0.21875),
        "second_bias": normal_values(seeds[6], (CH,), 0.5, 3.0, (), jnp.float32),
    }


def convolve_blocks(field, weight, biases):
    channels, extent_z, extent_x, extent_y = field.shape
    block_span = math.gcd(extent_z, 32)
    padded = jnp.pad(field.astype(jnp.float32), ((0, 0), (1, 1), (1, 1), (0, 0)))
    weight_wide = weight.astype(jnp.float32)

    def one_block(block_index):
        start = (block_index * block_span).astype(jnp.int32)
        window = lax.dynamic_slice(padded, (jnp.int32(0), start, jnp.int32(0), jnp.int32(0)), (channels, block_span + 2, extent_x + 2, extent_y))
        result = lax.conv_general_dilated(window[None], weight_wide, (1, 1, 1), ((0, 0), (0, 0), (1, 1)), dimension_numbers=("NCDHW", "OIDHW", "NCDHW"), precision=lax.Precision.HIGHEST)[0]
        return jnp.maximum(result + biases[:, None, None, None], 0.0).astype(jnp.bfloat16)

    blocks = lax.map(one_block, jnp.arange(extent_z // block_span, dtype=jnp.int32))
    return jnp.moveaxis(blocks, 0, 1).reshape(weight.shape[0], extent_z, extent_x, extent_y)


def reference(source_field, receiver_field, shot_group, first_weight, first_bias, second_weight, second_bias):
    total_shots = source_field.shape[0]
    labels = jnp.arange(GROUPS, dtype=jnp.int32)
    image_sum = jnp.zeros((GROUPS,) + source_field.shape[2:], jnp.float32)
    for shot_index in range(total_shots):
        cross_term = jnp.einsum("tzxy,tzxy->zxy", source_field[shot_index].astype(jnp.float32), receiver_field[shot_index].astype(jnp.float32))
        member = (labels == shot_group[shot_index]).astype(jnp.float32)
        image_sum = image_sum + member[:, None, None, None] * cross_term[None]
    image_tile = image_sum.astype(jnp.bfloat16)
    hidden = convolve_blocks(image_tile, first_weight, first_bias)
    return convolve_blocks(hidden, second_weight, second_bias)
```

```python
import functools

import jax
import jax.numpy as jnp
from jax import lax
from jax.experimental import pallas as pl
from jax.experimental.pallas import tpu as pltpu
from jax.sharding import PartitionSpec as P

WIDE = 6
OUT = 8


def extended(block, sides, width):
    for axis, dim in sides:
        count = lax.axis_size(axis)
        forward = [(i, i + 1) for i in range(count - 1)]
        backward = [(target, source) for source, target in forward]
        low = lax.ppermute(
            lax.slice_in_dim(block, block.shape[dim] - width, None, axis=dim), axis, forward
        )
        high = lax.ppermute(lax.slice_in_dim(block, 0, width, axis=dim), axis, backward)
        block = jnp.concatenate([low, block, high], axis=dim)
    return block


def banded(weight, count):
    rows = [
        jnp.pad(weight, ((0, 0), (0, 0), (i, count - 1 - i), (0, 0))) for i in range(count)
    ]
    return jnp.stack(rows), rows[0].shape[1] * rows[0].shape[2] * rows[0].shape[3]


def conv_kernel(tile_z, tile_x, shot_count, slab_count, place, img, w1, b1, w2, b2, out, wide, hidden):
    half = tile_z // 2
    y = img.shape[3]
    lanes = 2 * y
    lane = lax.broadcasted_iota(jnp.int32, (1, lanes), 1)
    upper = (lane >= y).astype(jnp.int32)
    cell = lane - upper * y
    first = cell == 0
    last = cell == y - 1
    channels = w1.shape[0] // WIDE

    def three(values):
        left = jnp.where(first, 0.0, pltpu.roll(values, 1, 1))
        right = jnp.where(last, 0.0, pltpu.roll(values, lanes - 1, 1))
        return [v.astype(jnp.bfloat16) for v in (left, values, right)]

    depth = img.shape[2]

    @pl.loop(0, half + 4)
    def _(z):
        for x in range(img.shape[1]):
            pair = jnp.concatenate(
                [img[z, x].astype(jnp.float32), img[z + half, x].astype(jnp.float32)], axis=1
            )
            for k, part in enumerate(three(pair)):
                wide[z, x, k * depth:(k + 1) * depth, :] = part

    z_base = place[0] * tile_z - 1
    x_base = place[1] * tile_x - 1
    hidden_x = hidden.shape[1]

    @pl.loop(0, half + 2)
    def _(z):
        z_place = z_base + z + upper * half
        z_valid = jnp.logical_and(z_place >= 0, z_place < tile_z * shot_count)
        for g in range(hidden_x // WIDE):
            window = wide[pl.ds(z, 3), g * WIDE:g * WIDE + WIDE + 2]
            got = jnp.dot(
                w1[...], window.reshape(-1, lanes), preferred_element_type=jnp.float32
            )
            for i in range(WIDE):
                x = g * WIDE + i
                x_place = x_base + x
                x_valid = jnp.logical_and(x_place >= 0, x_place < tile_x * slab_count)
                valid = jnp.logical_and(z_valid, x_valid)
                value = jnp.maximum(got[i * channels:(i + 1) * channels] + b1[...], 0.0)
                value = jnp.where(valid, value, 0.0)
                for k, part in enumerate(three(value)):
                    hidden[z, x, k * channels:(k + 1) * channels, :] = part

    out_channels = out.shape[0]
    chunk = min(16, tile_x)

    @pl.loop(0, half)
    def _(z):
        for c in range(tile_x // chunk):
            parts = []
            for g in range(chunk // OUT):
                x = c * chunk + g * OUT
                window = hidden[pl.ds(z, 3), x:x + OUT + 2]
                got = jnp.dot(
                    w2[...], window.reshape(-1, lanes), preferred_element_type=jnp.float32
                )
                parts.append(jnp.maximum(got + b2[...], 0.0))
            for h in range(2):
                pieces = [
                    p[:, h * y:(h + 1) * y].reshape(out_channels, OUT, y) for p in parts
                ]
                block = pieces[0] if len(pieces) == 1 else jnp.concatenate(pieces, axis=1)
                out[:, z + h * half, c * chunk:(c + 1) * chunk, :] = block.astype(out.dtype)


def convolutions(image, first_weight, first_bias, second_weight, second_bias, tile_z, tile_x):
    shot_count, slab_count = lax.axis_size("shot"), lax.axis_size("slab")
    channels, inputs = first_weight.shape[:2]
    out_channels = second_weight.shape[0]
    y = image.shape[3]
    depth = image.shape[2]
    half = tile_z // 2
    hidden_x = -(-(tile_x + 2) // WIDE) * WIDE
    w1 = jnp.transpose(first_weight, (0, 2, 3, 4, 1))
    w1 = jnp.pad(w1, ((0, 0),) * 4 + ((0, depth - inputs),)).reshape(channels, 3, 3, 3 * depth)
    w1, k1 = banded(w1, WIDE)
    w1 = w1.reshape(WIDE * channels, k1)
    w2 = jnp.transpose(second_weight, (0, 2, 3, 4, 1)).reshape(out_channels, 3, 3, 3 * channels)
    w2, k2 = banded(w2, OUT)
    w2 = jnp.transpose(w2, (1, 0, 2, 3, 4)).reshape(out_channels * OUT, k2)
    b1 = first_bias[:, None]
    b2 = jnp.repeat(second_bias, OUT)[:, None]
    place = jnp.stack([lax.axis_index("shot"), lax.axis_index("slab")]).astype(jnp.int32)
    vmem = pl.BlockSpec(memory_space=pltpu.VMEM)
    return pl.pallas_call(
        functools.partial(conv_kernel, tile_z, tile_x, shot_count, slab_count),
        out_shape=jax.ShapeDtypeStruct((out_channels, tile_z, tile_x, y), jnp.bfloat16),
        in_specs=[pl.BlockSpec(memory_space=pltpu.SMEM)] + [vmem] * 5,
        out_specs=vmem,
        scratch_shapes=[
            pltpu.VMEM((half + 4, image.shape[1], 3 * depth, 2 * y), jnp.bfloat16),
            pltpu.VMEM((half + 2, hidden_x, 3 * channels, 2 * y), jnp.bfloat16),
        ],
        compiler_params=pltpu.CompilerParams(vmem_limit_bytes=48 * 1024 * 1024),
        name="convolutions",
    )(place, image, w1, b1, w2, b2)


def shards(
    source_field, receiver_field, shot_group, first_weight, first_bias, second_weight, second_bias
):
    shots_here, _, slab_z, all_x, _ = source_field.shape
    shot_count, slab_count = lax.axis_size("shot"), lax.axis_size("slab")
    tile_z = slab_z * slab_count // shot_count
    tile_x = all_x // slab_count
    cross = jnp.sum(
        source_field.astype(jnp.float32) * receiver_field.astype(jnp.float32), axis=1
    ).astype(jnp.bfloat16)
    rows = lax.all_to_all(cross, "slab", split_axis=2, concat_axis=1, tiled=True)
    tile = lax.all_to_all(rows, "shot", split_axis=1, concat_axis=0, tiled=True)
    padded = extended(tile, (("shot", 1), ("slab", 2)), 2)
    hidden_x = -(-(tile_x + 2) // WIDE) * WIDE
    image = jnp.transpose(padded, (1, 2, 0, 3))
    shots = image.shape[2]
    depth = -(-shots // 16) * 16
    image = jnp.pad(
        image, ((0, 0), (0, hidden_x + 2 - image.shape[1]), (0, depth - shots), (0, 0))
    )
    weight_of_shot = jnp.take(first_weight, shot_group, axis=1)
    return convolutions(
        image, weight_of_shot, first_bias, second_weight, second_bias, tile_z, tile_x
    )


def solution(mesh):
    placed = (
        P("shot", None, "slab", None, None),
        P("shot", None, "slab", None, None),
        P(),
        P(),
        P(),
        P(),
        P(),
    )
    return jax.shard_map(
        shards, mesh=mesh, in_specs=placed, out_specs=P(None, "shot", "slab", None), check_vma=False
    )
```

```python
import functools

import jax
import jax.numpy as jnp
from jax import lax
from jax.experimental import pallas as pl
from jax.experimental.pallas import tpu as pltpu
from jax.sharding import PartitionSpec as P

WIDE = 6
OUT = 8


def exchange_kernel(shot_count, slab_count, slab_z, sent, got, send_sem, recv_sem, side_send, side_recv):
    shot, slab = lax.axis_index("shot"), lax.axis_index("slab")
    per_tile = slab_count // shot_count
    tile_z = slab_z * per_tile
    owner = slab // per_tile
    mine = slab % per_tile

    def place(shot_at, slab_at):
        return {"shot": shot_at, "slab": slab_at}

    def is_me(shot_at, slab_at):
        return jnp.logical_and(shot_at == shot, slab_at == slab)

    barrier = pltpu.get_barrier_semaphore()

    def greet(shot_at, slab_at):
        pl.semaphore_signal(
            barrier, inc=1, device_id=place(shot_at, slab_at), device_id_type=pl.DeviceIdType.MESH
        )

    for source in range(shot_count):
        for r in range(per_tile):
            source_slab = shot * per_tile + r

            @pl.when(jnp.logical_not(is_me(source, source_slab)))
            def _():
                greet(source, source_slab)

    @pl.when(shot > 0)
    def _():
        greet(shot - 1, slab)

    @pl.when(shot < shot_count - 1)
    def _():
        greet(shot + 1, slab)

    partners = (
        slab_count
        - (owner == shot).astype(jnp.int32)
        + (shot > 0).astype(jnp.int32)
        + (shot < shot_count - 1).astype(jnp.int32)
    )
    pl.semaphore_wait(barrier, partners)

    def slot(source, r):
        return got.at[source, pl.ds(2 + r * slab_z, slab_z)]

    def remote(k):
        target = lax.rem(slab + slab_count // 2 + k, slab_count)
        copy = pltpu.make_async_remote_copy(
            src_ref=sent.at[target],
            dst_ref=slot(shot, mine),
            send_sem=send_sem.at[k],
            recv_sem=recv_sem.at[shot, mine],
            device_id=place(owner, target),
            device_id_type=pl.DeviceIdType.MESH,
        )
        return target, copy

    def local(target):
        return pltpu.make_async_copy(
            sent.at[target], slot(shot, mine), recv_sem.at[shot, mine]
        )

    for k in range(slab_count):
        target, copy = remote(k)
        self_copy = is_me(owner, target)

        @pl.when(jnp.logical_not(self_copy))
        def _():
            copy.start()

        @pl.when(self_copy)
        def _():
            local(target).start()

    def arrived(r):
        for source in range(shot_count):
            pltpu.make_async_copy(slot(source, r), slot(source, r), recv_sem.at[source, r]).wait()

    def side(low):
        start, end = (2, tile_z + 2) if low else (tile_z, 0)
        index = 0 if low else 1
        return pltpu.make_async_remote_copy(
            src_ref=got.at[:, pl.ds(start, 2)],
            dst_ref=got.at[:, pl.ds(end, 2)],
            send_sem=side_send.at[index],
            recv_sem=side_recv.at[index],
            device_id=place(shot - 1 if low else shot + 1, slab),
            device_id_type=pl.DeviceIdType.MESH,
        )

    has_low, has_high = shot > 0, shot < shot_count - 1
    arrived(0)

    @pl.when(has_low)
    def _():
        side(True).start()

    for r in range(1, per_tile):
        arrived(r)

    @pl.when(has_high)
    def _():
        side(False).start()

    for k in range(slab_count):
        target, copy = remote(k)

        @pl.when(jnp.logical_not(is_me(owner, target)))
        def _():
            copy.wait_send()

    @pl.when(has_low)
    def _():
        side(True).wait_send()
        low = got.at[:, pl.ds(0, 2)]
        pltpu.make_async_copy(low, low, side_recv.at[1]).wait()

    @pl.when(has_high)
    def _():
        side(False).wait_send()
        high = got.at[:, pl.ds(tile_z + 2, 2)]
        pltpu.make_async_copy(high, high, side_recv.at[0]).wait()


def exchange(sent, slab_z):
    shot_count, slab_count = lax.axis_size("shot"), lax.axis_size("slab")
    per_tile = slab_count // shot_count
    tile_z = slab_z * per_tile
    anywhere = pl.BlockSpec(memory_space=pl.ANY)
    return pl.pallas_call(
        functools.partial(exchange_kernel, shot_count, slab_count, slab_z),
        out_shape=jax.ShapeDtypeStruct(
            (shot_count, tile_z + 4) + sent.shape[2:], jnp.bfloat16
        ),
        in_specs=[anywhere],
        out_specs=anywhere,
        scratch_shapes=[
            pltpu.SemaphoreType.DMA((slab_count,)),
            pltpu.SemaphoreType.DMA((shot_count, per_tile)),
            pltpu.SemaphoreType.DMA((2,)),
            pltpu.SemaphoreType.DMA((2,)),
        ],
        compiler_params=pltpu.CompilerParams(collective_id=0, has_side_effects=True),
        name="exchange",
    )(sent)


def spread(weight, count, lanes):
    base = jnp.pad(weight, ((0, 0), (0, 0), (0, count - 1), (0, 0)))
    base = base.reshape(base.shape[0], -1).astype(jnp.float32)
    return jnp.pad(base, ((0, 0), (0, lanes - base.shape[1])))


def lanes_for(size):
    return -(-size // 128) * 128


def banded(base, count, step):
    rows = [base] + [pltpu.roll(base, i * step, 1) for i in range(1, count)]
    return jnp.concatenate([r.astype(jnp.bfloat16) for r in rows], axis=0)


def conv_kernel(tile_z, tile_x, shot_count, slab_count, place, img, base1, b1, base2, b2, out, wide, hidden, w1, w2):
    half = tile_z // 2
    y = img.shape[3]
    lanes = 2 * y
    lane = lax.broadcasted_iota(jnp.int32, (1, lanes), 1)
    upper = (lane >= y).astype(jnp.int32)
    cell = lane - upper * y
    first = cell == 0
    last = cell == y - 1
    channels = base1.shape[0]
    out_channels = out.shape[0]
    w1[...] = banded(base1[...], WIDE, 3 * img.shape[2])[:, : w1.shape[1]]
    rows = banded(base2[...], OUT, 3 * channels)
    count = rows.shape[0]
    to = lax.broadcasted_iota(jnp.int32, (count, count), 0)
    source = lax.broadcasted_iota(jnp.int32, (count, count), 1)
    moved = (to % OUT) * out_channels + to // OUT == source
    swap = jnp.where(moved, 1.0, 0.0).astype(jnp.bfloat16)
    w2[...] = jnp.dot(swap, rows, preferred_element_type=jnp.float32).astype(jnp.bfloat16)[
        :, : w2.shape[1]
    ]

    def three(values):
        left = jnp.where(first, 0.0, pltpu.roll(values, 1, 1))
        right = jnp.where(last, 0.0, pltpu.roll(values, lanes - 1, 1))
        return [v.astype(jnp.bfloat16) for v in (left, values, right)]

    depth = img.shape[2]

    @pl.loop(0, half + 4)
    def _(z):
        for x in range(img.shape[1]):
            pair = jnp.concatenate(
                [img[z, x].astype(jnp.float32), img[z + half, x].astype(jnp.float32)], axis=1
            )
            for k, part in enumerate(three(pair)):
                wide[z, x, k * depth:(k + 1) * depth, :] = part

    z_base = place[0] * tile_z - 1
    x_base = place[1] * tile_x - 1
    hidden_x = hidden.shape[1]

    @pl.loop(0, half + 2)
    def _(z):
        z_place = z_base + z + upper * half
        z_valid = jnp.logical_and(z_place >= 0, z_place < tile_z * shot_count)
        for g in range(hidden_x // WIDE):
            window = wide[pl.ds(z, 3), g * WIDE:g * WIDE + WIDE + 2]
            got = jnp.dot(
                w1[...], window.reshape(-1, lanes), preferred_element_type=jnp.float32
            )
            for i in range(WIDE):
                x = g * WIDE + i
                x_place = x_base + x
                x_valid = jnp.logical_and(x_place >= 0, x_place < tile_x * slab_count)
                valid = jnp.logical_and(z_valid, x_valid)
                value = jnp.maximum(got[i * channels:(i + 1) * channels] + b1[...], 0.0)
                value = jnp.where(valid, value, 0.0)
                for k, part in enumerate(three(value)):
                    hidden[z, x, k * channels:(k + 1) * channels, :] = part

    chunk = min(16, tile_x)

    @pl.loop(0, half)
    def _(z):
        for c in range(tile_x // chunk):
            parts = []
            for g in range(chunk // OUT):
                x = c * chunk + g * OUT
                window = hidden[pl.ds(z, 3), x:x + OUT + 2]
                got = jnp.dot(
                    w2[...], window.reshape(-1, lanes), preferred_element_type=jnp.float32
                )
                parts.append(jnp.maximum(got + b2[...], 0.0))
            for h in range(2):
                pieces = [
                    p[:, h * y:(h + 1) * y].reshape(out_channels, OUT, y) for p in parts
                ]
                block = pieces[0] if len(pieces) == 1 else jnp.concatenate(pieces, axis=1)
                out[:, z + h * half, c * chunk:(c + 1) * chunk, :] = block.astype(out.dtype)


def convolutions(image, first_weight, first_bias, second_weight, second_bias, tile_z, tile_x):
    shot_count, slab_count = lax.axis_size("shot"), lax.axis_size("slab")
    channels, inputs = first_weight.shape[:2]
    out_channels = second_weight.shape[0]
    y = image.shape[3]
    depth = image.shape[2]
    half = tile_z // 2
    hidden_x = -(-(tile_x + 2) // WIDE) * WIDE
    w1 = jnp.transpose(first_weight, (0, 2, 3, 4, 1))
    w1 = jnp.pad(w1, ((0, 0),) * 4 + ((0, depth - inputs),)).reshape(channels, 3, 3, 3 * depth)
    k1 = 3 * (WIDE + 2) * 3 * depth
    w1 = spread(w1, WIDE, lanes_for(k1))
    w2 = jnp.transpose(second_weight, (0, 2, 3, 4, 1)).reshape(out_channels, 3, 3, 3 * channels)
    k2 = 3 * (OUT + 2) * 3 * channels
    w2 = spread(w2, OUT, lanes_for(k2))
    b1 = first_bias[:, None]
    b2 = jnp.repeat(second_bias, OUT)[:, None]
    place = jnp.stack([lax.axis_index("shot"), lax.axis_index("slab")]).astype(jnp.int32)
    vmem = pl.BlockSpec(memory_space=pltpu.VMEM)
    return pl.pallas_call(
        functools.partial(conv_kernel, tile_z, tile_x, shot_count, slab_count),
        out_shape=jax.ShapeDtypeStruct((out_channels, tile_z, tile_x, y), jnp.bfloat16),
        in_specs=[pl.BlockSpec(memory_space=pltpu.SMEM)] + [vmem] * 5,
        out_specs=vmem,
        scratch_shapes=[
            pltpu.VMEM((half + 4, image.shape[1], 3 * depth, 2 * y), jnp.bfloat16),
            pltpu.VMEM((half + 2, hidden_x, 3 * channels, 2 * y), jnp.bfloat16),
            pltpu.VMEM((WIDE * channels, k1), jnp.bfloat16),
            pltpu.VMEM((OUT * out_channels, k2), jnp.bfloat16),
        ],
        compiler_params=pltpu.CompilerParams(vmem_limit_bytes=48 * 1024 * 1024),
        name="convolutions",
    )(place, image, w1, b1, w2, b2)


def shards(
    source_field, receiver_field, shot_group, first_weight, first_bias, second_weight, second_bias
):
    shots_here, _, slab_z, all_x, _ = source_field.shape
    shot_count, slab_count = lax.axis_size("shot"), lax.axis_size("slab")
    tile_z = slab_z * slab_count // shot_count
    tile_x = all_x // slab_count
    cross = jnp.sum(
        source_field.astype(jnp.float32) * receiver_field.astype(jnp.float32), axis=1
    ).astype(jnp.bfloat16)
    wide_x = tile_x + 4
    cross = jnp.pad(cross, ((0, 0), (0, 0), (2, 2), (0, 0)))
    tiles = jnp.stack(
        [cross[:, :, t * tile_x:t * tile_x + wide_x] for t in range(slab_count)]
    )
    packed = shots_here * wide_x
    spare = -(-packed // 16) * 16 - packed
    sent = jnp.transpose(tiles, (0, 2, 1, 3, 4)).reshape(slab_count, slab_z, packed, -1)
    sent = jnp.pad(sent, ((0, 0), (0, 0), (0, spare), (0, 0)))
    got = exchange(sent, slab_z)[:, :, :packed]
    z_place = lax.axis_index("shot") * tile_z - 2 + jnp.arange(tile_z + 4, dtype=jnp.int32)
    z_valid = (z_place >= 0) & (z_place < tile_z * shot_count)
    got = jnp.where(z_valid[None, :, None, None], got, jnp.zeros_like(got))
    got = got.reshape(shot_count, tile_z + 4, shots_here, wide_x, -1)
    shots = shot_count * shots_here
    image = jnp.transpose(got, (1, 3, 0, 2, 4)).reshape(tile_z + 4, wide_x, shots, -1)
    hidden_x = -(-(tile_x + 2) // WIDE) * WIDE
    depth = -(-shots // 16) * 16
    image = jnp.pad(
        image, ((0, 0), (0, hidden_x + 2 - wide_x), (0, depth - shots), (0, 0))
    )
    weight_of_shot = jnp.take(first_weight, shot_group, axis=1)
    return convolutions(
        image, weight_of_shot, first_bias, second_weight, second_bias, tile_z, tile_x
    )


def solution(mesh):
    placed = (
        P("shot", None, "slab", None, None),
        P("shot", None, "slab", None, None),
        P(),
        P(),
        P(),
        P(),
        P(),
    )
    return jax.shard_map(
        shards, mesh=mesh, in_specs=placed, out_specs=P(None, "shot", "slab", None), check_vma=False
    )
```

```python
import functools

import jax
import jax.numpy as jnp
from jax import lax
from jax.experimental import pallas as pl
from jax.experimental.pallas import tpu as pltpu
from jax.sharding import PartitionSpec as P

WIDE = 6
OUT = 8


def exchange_kernel(
    shot_count, slab_count, tile_x, source, receiver, got,
    source_part, receiver_part, edged, sent, load_sem, send_sem, recv_sem, side_send, side_recv,
):
    shots_here, steps, slab_z, all_x, _ = source.shape
    chunk_x = source_part.shape[4]
    per_chunk = chunk_x // tile_x
    chunks = all_x // chunk_x
    wide_x = tile_x + 4
    shot, slab = lax.axis_index("shot"), lax.axis_index("slab")
    per_tile = slab_count // shot_count
    tile_z = slab_z * per_tile
    owner = slab // per_tile
    mine = slab % per_tile

    def place(shot_at, slab_at):
        return {"shot": shot_at, "slab": slab_at}

    def is_me(shot_at, slab_at):
        return jnp.logical_and(shot_at == shot, slab_at == slab)

    def chunk_at(k):
        return lax.rem(slab // per_chunk + chunks // 2 - 1 + k, chunks)

    def loads(k):
        rows = pl.ds(pl.multiple_of(chunk_at(k) * chunk_x, chunk_x), chunk_x)
        return [
            pltpu.make_async_copy(
                field.at[:, :, :, rows], part.at[k], load_sem.at[i, k]
            )
            for i, (field, part) in enumerate(
                ((source, source_part), (receiver, receiver_part))
            )
        ]

    for k in range(chunks):
        for copy in loads(k):
            copy.start()

    barrier = pltpu.get_barrier_semaphore()

    def greet(shot_at, slab_at):
        pl.semaphore_signal(
            barrier, inc=1, device_id=place(shot_at, slab_at), device_id_type=pl.DeviceIdType.MESH
        )

    for from_shot in range(shot_count):
        for r in range(per_tile):
            from_slab = shot * per_tile + r

            @pl.when(jnp.logical_not(is_me(from_shot, from_slab)))
            def _():
                greet(from_shot, from_slab)

    @pl.when(shot > 0)
    def _():
        greet(shot - 1, slab)

    @pl.when(shot < shot_count - 1)
    def _():
        greet(shot + 1, slab)

    partners = (
        slab_count
        - (owner == shot).astype(jnp.int32)
        + (shot > 0).astype(jnp.int32)
        + (shot < shot_count - 1).astype(jnp.int32)
    )
    pl.semaphore_wait(barrier, partners)

    def slot(from_shot, r):
        return got.at[from_shot, pl.ds(2 + r * slab_z, slab_z)]

    def remote(n):
        target = chunk_at(n // per_chunk) * per_chunk + n % per_chunk
        copy = pltpu.make_async_remote_copy(
            src_ref=sent.at[n],
            dst_ref=slot(shot, mine),
            send_sem=send_sem.at[n],
            recv_sem=recv_sem.at[shot, mine],
            device_id=place(owner, target),
            device_id_type=pl.DeviceIdType.MESH,
        )
        return target, copy

    def multiply(k):
        for copy in loads(k):
            copy.wait()
        first = chunk_at(k) * per_chunk + 1

        @pl.loop(0, slab_z)
        def _(z):
            for l in range(shots_here):
                total = None
                for t in range(steps):
                    term = source_part[k, l, t, z].astype(jnp.float32) * receiver_part[
                        k, l, t, z
                    ].astype(jnp.float32)
                    total = term if total is None else total + term
                row = l * wide_x
                for j in range(per_chunk):
                    part = total[j * tile_x:(j + 1) * tile_x]
                    edged[first + j, z, row + 2:row + 2 + tile_x] = part
                    edged[first + j + 1, z, row:row + 2] = part[tile_x - 2:]
                    edged[first + j - 1, z, row + 2 + tile_x:row + wide_x] = part[:2]

    def send(k):
        for j in range(per_chunk):
            n = k * per_chunk + j
            target, copy = remote(n)

            @pl.loop(0, slab_z)
            def _(z):
                sent[n, z] = edged[target + 1, z].astype(sent.dtype)

            self_copy = is_me(owner, target)

            @pl.when(jnp.logical_not(self_copy))
            def _():
                copy.start()

            @pl.when(self_copy)
            def _():
                pltpu.make_async_copy(
                    sent.at[n], slot(shot, mine), recv_sem.at[shot, mine]
                ).start()

    for z in range(slab_z):
        edged[:, z] = jnp.zeros_like(edged[:, z])
    for k in range(chunks):
        multiply(k)
        if k >= 2:
            send(k - 1)
    send(chunks - 1)
    send(0)

    def arrived(r):
        for from_shot in range(shot_count):
            here = slot(from_shot, r)
            pltpu.make_async_copy(here, here, recv_sem.at[from_shot, r]).wait()

    def side(low):
        start, end = (2, tile_z + 2) if low else (tile_z, 0)
        index = 0 if low else 1
        return pltpu.make_async_remote_copy(
            src_ref=got.at[:, pl.ds(start, 2)],
            dst_ref=got.at[:, pl.ds(end, 2)],
            send_sem=side_send.at[index],
            recv_sem=side_recv.at[index],
            device_id=place(shot - 1 if low else shot + 1, slab),
            device_id_type=pl.DeviceIdType.MESH,
        )

    has_low, has_high = shot > 0, shot < shot_count - 1
    arrived(0)

    @pl.when(has_low)
    def _():
        side(True).start()

    for r in range(1, per_tile):
        arrived(r)

    @pl.when(has_high)
    def _():
        side(False).start()

    for n in range(slab_count):
        target, copy = remote(n)

        @pl.when(jnp.logical_not(is_me(owner, target)))
        def _():
            copy.wait_send()

    @pl.when(has_low)
    def _():
        side(True).wait_send()
        low = got.at[:, pl.ds(0, 2)]
        pltpu.make_async_copy(low, low, side_recv.at[1]).wait()

    @pl.when(has_high)
    def _():
        side(False).wait_send()
        high = got.at[:, pl.ds(tile_z + 2, 2)]
        pltpu.make_async_copy(high, high, side_recv.at[0]).wait()


def exchange(source, receiver):
    shots_here, steps, slab_z, all_x, y = source.shape
    shot_count, slab_count = lax.axis_size("shot"), lax.axis_size("slab")
    per_tile = slab_count // shot_count
    tile_z = slab_z * per_tile
    tile_x = all_x // slab_count
    chunk_x = max(tile_x, 16)
    chunks = all_x // chunk_x
    packed = -(-shots_here * (tile_x + 4) // 16) * 16
    anywhere = pl.BlockSpec(memory_space=pl.ANY)
    part = pltpu.VMEM((chunks, shots_here, steps, slab_z, chunk_x, y), jnp.bfloat16)
    return pl.pallas_call(
        functools.partial(exchange_kernel, shot_count, slab_count, tile_x),
        out_shape=jax.ShapeDtypeStruct((shot_count, tile_z + 4, packed, y), jnp.bfloat16),
        in_specs=[anywhere] * 2,
        out_specs=anywhere,
        scratch_shapes=[
            part,
            part,
            pltpu.VMEM((slab_count + 2, slab_z, packed, y), jnp.float32),
            pltpu.VMEM((slab_count, slab_z, packed, y), jnp.bfloat16),
            pltpu.SemaphoreType.DMA((2, chunks)),
            pltpu.SemaphoreType.DMA((slab_count,)),
            pltpu.SemaphoreType.DMA((shot_count, per_tile)),
            pltpu.SemaphoreType.DMA((2,)),
            pltpu.SemaphoreType.DMA((2,)),
        ],
        compiler_params=pltpu.CompilerParams(
            collective_id=0, has_side_effects=True, vmem_limit_bytes=56 * 1024 * 1024
        ),
        name="exchange",
    )(source, receiver)


def spread(weight, count, lanes):
    base = jnp.pad(weight, ((0, 0), (0, 0), (0, count - 1), (0, 0)))
    base = base.reshape(base.shape[0], -1).astype(jnp.float32)
    return jnp.pad(base, ((0, 0), (0, lanes - base.shape[1])))


def lanes_for(size):
    return -(-size // 128) * 128


def column(row, repeats):
    count = row.shape[1]
    to = lax.broadcasted_iota(jnp.int32, (count * repeats, count), 0) // repeats
    source = lax.broadcasted_iota(jnp.int32, (count * repeats, count), 1)
    return jnp.sum(jnp.where(to == source, row, 0.0), axis=1, keepdims=True)


def banded(base, count, step):
    rows = [base] + [pltpu.roll(base, i * step, 1) for i in range(1, count)]
    return jnp.concatenate([r.astype(jnp.bfloat16) for r in rows], axis=0)


def conv_kernel(tile_z, tile_x, shot_count, slab_count, place, img, base1, bias1, base2, bias2, out, wide, hidden, w1, w2):
    half = tile_z // 2
    y = img.shape[3]
    lanes = 2 * y
    lane = lax.broadcasted_iota(jnp.int32, (1, lanes), 1)
    upper = (lane >= y).astype(jnp.int32)
    cell = lane - upper * y
    first = cell == 0
    last = cell == y - 1
    channels = base1.shape[0]
    out_channels = out.shape[0]
    w1[...] = banded(base1[...], WIDE, 3 * img.shape[2])[:, : w1.shape[1]]
    b1 = column(bias1[...], 1)
    b2 = column(bias2[...], OUT)
    rows = banded(base2[...], OUT, 3 * channels)
    count = rows.shape[0]
    to = lax.broadcasted_iota(jnp.int32, (count, count), 0)
    source = lax.broadcasted_iota(jnp.int32, (count, count), 1)
    moved = (to % OUT) * out_channels + to // OUT == source
    swap = jnp.where(moved, 1.0, 0.0).astype(jnp.bfloat16)
    w2[...] = jnp.dot(swap, rows, preferred_element_type=jnp.float32).astype(jnp.bfloat16)[
        :, : w2.shape[1]
    ]

    def three(values):
        left = jnp.where(first, 0.0, pltpu.roll(values, 1, 1))
        right = jnp.where(last, 0.0, pltpu.roll(values, lanes - 1, 1))
        return [v.astype(jnp.bfloat16) for v in (left, values, right)]

    depth = img.shape[2]

    @pl.loop(0, half + 4)
    def _(z):
        for x in range(img.shape[1]):
            pair = jnp.concatenate(
                [img[z, x].astype(jnp.float32), img[z + half, x].astype(jnp.float32)], axis=1
            )
            for k, part in enumerate(three(pair)):
                wide[z, x, k * depth:(k + 1) * depth, :] = part

    z_base = place[0] * tile_z - 1
    x_base = place[1] * tile_x - 1
    hidden_x = hidden.shape[1]

    @pl.loop(0, half + 2)
    def _(z):
        z_place = z_base + z + upper * half
        z_valid = jnp.logical_and(z_place >= 0, z_place < tile_z * shot_count)
        for g in range(hidden_x // WIDE):
            window = wide[pl.ds(z, 3), g * WIDE:g * WIDE + WIDE + 2]
            got = jnp.dot(
                w1[...], window.reshape(-1, lanes), preferred_element_type=jnp.float32
            )
            for i in range(WIDE):
                x = g * WIDE + i
                x_place = x_base + x
                x_valid = jnp.logical_and(x_place >= 0, x_place < tile_x * slab_count)
                valid = jnp.logical_and(z_valid, x_valid)
                value = jnp.maximum(got[i * channels:(i + 1) * channels] + b1, 0.0)
                value = jnp.where(valid, value, 0.0)
                for k, part in enumerate(three(value)):
                    hidden[z, x, k * channels:(k + 1) * channels, :] = part

    chunk = min(16, tile_x)

    @pl.loop(0, half)
    def _(z):
        for c in range(tile_x // chunk):
            parts = []
            for g in range(chunk // OUT):
                x = c * chunk + g * OUT
                window = hidden[pl.ds(z, 3), x:x + OUT + 2]
                got = jnp.dot(
                    w2[...], window.reshape(-1, lanes), preferred_element_type=jnp.float32
                )
                parts.append(jnp.maximum(got + b2, 0.0))
            for h in range(2):
                pieces = [
                    p[:, h * y:(h + 1) * y].reshape(out_channels, OUT, y) for p in parts
                ]
                block = pieces[0] if len(pieces) == 1 else jnp.concatenate(pieces, axis=1)
                out[:, z + h * half, c * chunk:(c + 1) * chunk, :] = block.astype(out.dtype)


def convolutions(image, first_weight, first_bias, second_weight, second_bias, tile_z, tile_x):
    shot_count, slab_count = lax.axis_size("shot"), lax.axis_size("slab")
    channels, inputs = first_weight.shape[:2]
    out_channels = second_weight.shape[0]
    y = image.shape[3]
    depth = image.shape[2]
    half = tile_z // 2
    hidden_x = -(-(tile_x + 2) // WIDE) * WIDE
    w1 = jnp.transpose(first_weight, (0, 2, 3, 4, 1))
    w1 = jnp.pad(w1, ((0, 0),) * 4 + ((0, depth - inputs),)).reshape(channels, 3, 3, 3 * depth)
    k1 = 3 * (WIDE + 2) * 3 * depth
    w1 = spread(w1, WIDE, lanes_for(k1))
    w2 = jnp.transpose(second_weight, (0, 2, 3, 4, 1)).reshape(out_channels, 3, 3, 3 * channels)
    k2 = 3 * (OUT + 2) * 3 * channels
    w2 = spread(w2, OUT, lanes_for(k2))
    b1 = first_bias[None]
    b2 = second_bias[None]
    place = jnp.stack([lax.axis_index("shot"), lax.axis_index("slab")]).astype(jnp.int32)
    vmem = pl.BlockSpec(memory_space=pltpu.VMEM)
    return pl.pallas_call(
        functools.partial(conv_kernel, tile_z, tile_x, shot_count, slab_count),
        out_shape=jax.ShapeDtypeStruct((out_channels, tile_z, tile_x, y), jnp.bfloat16),
        in_specs=[pl.BlockSpec(memory_space=pltpu.SMEM)] + [vmem] * 5,
        out_specs=vmem,
        scratch_shapes=[
            pltpu.VMEM((half + 4, image.shape[1], 3 * depth, 2 * y), jnp.bfloat16),
            pltpu.VMEM((half + 2, hidden_x, 3 * channels, 2 * y), jnp.bfloat16),
            pltpu.VMEM((WIDE * channels, k1), jnp.bfloat16),
            pltpu.VMEM((OUT * out_channels, k2), jnp.bfloat16),
        ],
        compiler_params=pltpu.CompilerParams(vmem_limit_bytes=48 * 1024 * 1024),
        name="convolutions",
    )(place, image, w1, b1, w2, b2)


def shards(
    source_field, receiver_field, shot_group, first_weight, first_bias, second_weight, second_bias
):
    shots_here, _, slab_z, all_x, _ = source_field.shape
    shot_count, slab_count = lax.axis_size("shot"), lax.axis_size("slab")
    tile_z = slab_z * slab_count // shot_count
    tile_x = all_x // slab_count
    wide_x = tile_x + 4
    packed = shots_here * wide_x
    got = exchange(source_field, receiver_field)[:, :, :packed]
    z_place = lax.axis_index("shot") * tile_z - 2 + jnp.arange(tile_z + 4, dtype=jnp.int32)
    z_valid = (z_place >= 0) & (z_place < tile_z * shot_count)
    got = jnp.where(z_valid[None, :, None, None], got, jnp.zeros_like(got))
    got = got.reshape(shot_count, tile_z + 4, shots_here, wide_x, -1)
    shots = shot_count * shots_here
    image = jnp.transpose(got, (1, 3, 0, 2, 4)).reshape(tile_z + 4, wide_x, shots, -1)
    hidden_x = -(-(tile_x + 2) // WIDE) * WIDE
    depth = -(-shots // 16) * 16
    image = jnp.pad(
        image, ((0, 0), (0, hidden_x + 2 - wide_x), (0, depth - shots), (0, 0))
    )
    weight_of_shot = first_weight.at[:, shot_group].get(mode="promise_in_bounds")
    return convolutions(
        image, weight_of_shot, first_bias, second_weight, second_bias, tile_z, tile_x
    )


def solution(mesh):
    placed = (
        P("shot", None, "slab", None, None),
        P("shot", None, "slab", None, None),
        P(),
        P(),
        P(),
        P(),
        P(),
    )
    return jax.shard_map(
        shards, mesh=mesh, in_specs=placed, out_specs=P(None, "shot", "slab", None), check_vma=False
    )
```

```python
import functools

import jax
import jax.numpy as jnp
from jax import lax
from jax.experimental import pallas as pl
from jax.experimental.pallas import tpu as pltpu
from jax.sharding import PartitionSpec as P

WIDE = 6
OUT = 8


def exchange_kernel(
    shot_count, slab_count, tile_x, source, receiver, got,
    source_part, receiver_part, edged, sent, load_sem, send_sem, recv_sem, side_send, side_recv,
):
    shots_here, steps, slab_z, all_x, _ = source.shape
    chunk_x = source_part.shape[4]
    per_chunk = chunk_x // tile_x
    chunks = all_x // chunk_x
    wide_x = tile_x + 4
    shot, slab = lax.axis_index("shot"), lax.axis_index("slab")
    per_tile = slab_count // shot_count
    tile_z = slab_z * per_tile
    owner = slab // per_tile
    mine = slab % per_tile

    def place(shot_at, slab_at):
        return {"shot": shot_at, "slab": slab_at}

    def is_me(shot_at, slab_at):
        return jnp.logical_and(shot_at == shot, slab_at == slab)

    def chunk_at(k):
        return lax.rem(slab // per_chunk + chunks // 2 - 1 + k, chunks)

    def loads(k):
        rows = pl.ds(pl.multiple_of(chunk_at(k) * chunk_x, chunk_x), chunk_x)
        return [
            pltpu.make_async_copy(
                field.at[:, :, :, rows], part.at[k], load_sem.at[i, k]
            )
            for i, (field, part) in enumerate(
                ((source, source_part), (receiver, receiver_part))
            )
        ]

    for k in range(chunks):
        for copy in loads(k):
            copy.start()

    barrier = pltpu.get_barrier_semaphore()

    def greet(shot_at, slab_at):
        pl.semaphore_signal(
            barrier, inc=1, device_id=place(shot_at, slab_at), device_id_type=pl.DeviceIdType.MESH
        )

    for from_shot in range(shot_count):
        for r in range(per_tile):
            from_slab = shot * per_tile + r

            @pl.when(jnp.logical_not(is_me(from_shot, from_slab)))
            def _():
                greet(from_shot, from_slab)

    @pl.when(shot > 0)
    def _():
        greet(shot - 1, slab)

    @pl.when(shot < shot_count - 1)
    def _():
        greet(shot + 1, slab)

    partners = (
        slab_count
        - (owner == shot).astype(jnp.int32)
        + (shot > 0).astype(jnp.int32)
        + (shot < shot_count - 1).astype(jnp.int32)
    )
    pl.semaphore_wait(barrier, partners)

    def slot(from_shot, r):
        return got.at[from_shot, pl.ds(2 + r * slab_z, slab_z)]

    def remote(n):
        target = chunk_at(n // per_chunk) * per_chunk + n % per_chunk
        copy = pltpu.make_async_remote_copy(
            src_ref=sent.at[n],
            dst_ref=slot(shot, mine),
            send_sem=send_sem.at[n],
            recv_sem=recv_sem.at[shot, mine],
            device_id=place(owner, target),
            device_id_type=pl.DeviceIdType.MESH,
        )
        return target, copy

    def multiply(k):
        for copy in loads(k):
            copy.wait()
        first = chunk_at(k) * per_chunk + 1

        @pl.loop(0, slab_z)
        def _(z):
            for l in range(shots_here):
                total = None
                for t in range(steps):
                    term = source_part[k, l, t, z].astype(jnp.float32) * receiver_part[
                        k, l, t, z
                    ].astype(jnp.float32)
                    total = term if total is None else total + term
                row = l * wide_x
                for j in range(per_chunk):
                    part = total[j * tile_x:(j + 1) * tile_x]
                    edged[first + j, z, row + 2:row + 2 + tile_x] = part
                    edged[first + j + 1, z, row:row + 2] = part[tile_x - 2:]
                    edged[first + j - 1, z, row + 2 + tile_x:row + wide_x] = part[:2]

    def send(k):
        for j in range(per_chunk):
            n = k * per_chunk + j
            target, copy = remote(n)

            @pl.loop(0, slab_z)
            def _(z):
                sent[n, z] = edged[target + 1, z].astype(sent.dtype)

            self_copy = is_me(owner, target)

            @pl.when(jnp.logical_not(self_copy))
            def _():
                copy.start()

            @pl.when(self_copy)
            def _():
                pltpu.make_async_copy(
                    sent.at[n], slot(shot, mine), recv_sem.at[shot, mine]
                ).start()

    for z in range(slab_z):
        edged[:, z] = jnp.zeros_like(edged[:, z])
    for k in range(chunks):
        multiply(k)
        if k >= 2:
            send(k - 1)
    send(chunks - 1)
    send(0)

    def arrived(r):
        for from_shot in range(shot_count):
            here = slot(from_shot, r)
            pltpu.make_async_copy(here, here, recv_sem.at[from_shot, r]).wait()

    def side(low):
        start, end = (2, tile_z + 2) if low else (tile_z, 0)
        index = 0 if low else 1
        return pltpu.make_async_remote_copy(
            src_ref=got.at[:, pl.ds(start, 2)],
            dst_ref=got.at[:, pl.ds(end, 2)],
            send_sem=side_send.at[index],
            recv_sem=side_recv.at[index],
            device_id=place(shot - 1 if low else shot + 1, slab),
            device_id_type=pl.DeviceIdType.MESH,
        )

    has_low, has_high = shot > 0, shot < shot_count - 1
    arrived(0)

    @pl.when(has_low)
    def _():
        side(True).start()

    for r in range(1, per_tile):
        arrived(r)

    @pl.when(has_high)
    def _():
        side(False).start()

    for n in range(slab_count):
        target, copy = remote(n)

        @pl.when(jnp.logical_not(is_me(owner, target)))
        def _():
            copy.wait_send()

    @pl.when(has_low)
    def _():
        side(True).wait_send()
        low = got.at[:, pl.ds(0, 2)]
        pltpu.make_async_copy(low, low, side_recv.at[1]).wait()

    @pl.when(has_high)
    def _():
        side(False).wait_send()
        high = got.at[:, pl.ds(tile_z + 2, 2)]
        pltpu.make_async_copy(high, high, side_recv.at[0]).wait()


def exchange(source, receiver):
    shots_here, steps, slab_z, all_x, y = source.shape
    shot_count, slab_count = lax.axis_size("shot"), lax.axis_size("slab")
    per_tile = slab_count // shot_count
    tile_z = slab_z * per_tile
    tile_x = all_x // slab_count
    chunk_x = max(tile_x, 16)
    chunks = all_x // chunk_x
    packed = -(-shots_here * (tile_x + 4) // 16) * 16
    anywhere = pl.BlockSpec(memory_space=pl.ANY)
    part = pltpu.VMEM((chunks, shots_here, steps, slab_z, chunk_x, y), jnp.bfloat16)
    return pl.pallas_call(
        functools.partial(exchange_kernel, shot_count, slab_count, tile_x),
        out_shape=jax.ShapeDtypeStruct((shot_count, tile_z + 4, packed, y), jnp.bfloat16),
        in_specs=[anywhere] * 2,
        out_specs=anywhere,
        scratch_shapes=[
            part,
            part,
            pltpu.VMEM((slab_count + 2, slab_z, packed, y), jnp.float32),
            pltpu.VMEM((slab_count, slab_z, packed, y), jnp.bfloat16),
            pltpu.SemaphoreType.DMA((2, chunks)),
            pltpu.SemaphoreType.DMA((slab_count,)),
            pltpu.SemaphoreType.DMA((shot_count, per_tile)),
            pltpu.SemaphoreType.DMA((2,)),
            pltpu.SemaphoreType.DMA((2,)),
        ],
        compiler_params=pltpu.CompilerParams(
            collective_id=0, has_side_effects=True, vmem_limit_bytes=56 * 1024 * 1024
        ),
        name="exchange",
    )(source, receiver)


def spread(weight, count, lanes):
    base = jnp.pad(weight, ((0, 0), (0, 0), (0, count - 1), (0, 0)))
    base = base.reshape(base.shape[0], -1).astype(jnp.float32)
    return jnp.pad(base, ((0, 0), (0, lanes - base.shape[1])))


def lanes_for(size):
    return -(-size // 128) * 128


def column(row, repeats):
    count = row.shape[1]
    to = lax.broadcasted_iota(jnp.int32, (count * repeats, count), 0) // repeats
    source = lax.broadcasted_iota(jnp.int32, (count * repeats, count), 1)
    return jnp.sum(jnp.where(to == source, row, 0.0), axis=1, keepdims=True)


def banded(base, count, step):
    rows = [base] + [pltpu.roll(base, i * step, 1) for i in range(1, count)]
    return jnp.concatenate([r.astype(jnp.bfloat16) for r in rows], axis=0)


def conv_kernel(
    tile_z, tile_x, shot_count, slab_count, shots_here,
    place, got, base1, bias1, base2, bias2, out, wide, hidden, w1, w2, plane,
):
    half = tile_z // 2
    y = got.shape[3]
    lanes = 2 * y
    lane = lax.broadcasted_iota(jnp.int32, (1, lanes), 1)
    upper = (lane >= y).astype(jnp.int32)
    cell = lane - upper * y
    first = cell == 0
    last = cell == y - 1
    channels = base1.shape[0]
    out_channels = out.shape[0]
    w1[...] = banded(base1[...], WIDE, 1)[:, : w1.shape[1]]
    b1 = column(bias1[...], 1)
    b2 = column(bias2[...], OUT)
    rows = banded(base2[...], OUT, 3 * channels)
    count = rows.shape[0]
    to = lax.broadcasted_iota(jnp.int32, (count, count), 0)
    source = lax.broadcasted_iota(jnp.int32, (count, count), 1)
    moved = (to % OUT) * out_channels + to // OUT == source
    swap = jnp.where(moved, 1.0, 0.0).astype(jnp.bfloat16)
    w2[...] = jnp.dot(swap, rows, preferred_element_type=jnp.float32).astype(jnp.bfloat16)[
        :, : w2.shape[1]
    ]

    def three(values):
        left = jnp.where(first, 0.0, pltpu.roll(values, 1, 1))
        right = jnp.where(last, 0.0, pltpu.roll(values, lanes - 1, 1))
        return [v.astype(jnp.bfloat16) for v in (left, values, right)]

    wide_x = tile_x + 4
    depth = wide.shape[2] // 3
    hidden_x = hidden.shape[1]

    @pl.loop(0, half + 4)
    def _(z):
        for h in range(2):
            z_at = place[0] * tile_z - 2 + z + h * half
            here = jnp.logical_and(z_at >= 0, z_at < tile_z * shot_count)
            for s in range(shot_count):
                rows = got[s, z + h * half].astype(jnp.float32)
                plane[h, s] = jnp.where(here, rows, 0.0)
        for g in range(hidden_x // WIDE):
            pieces = []
            for s in range(shot_count):
                for l in range(shots_here):
                    row = l * wide_x + g * WIDE
                    pieces.append(
                        jnp.concatenate(
                            [plane[h, s, row:row + WIDE + 2] for h in range(2)], axis=1
                        )
                    )
            for k, part in enumerate(three(jnp.concatenate(pieces, axis=0))):
                wide[z, g, k * depth:(k + 1) * depth, :] = part

    z_base = place[0] * tile_z - 1
    x_base = place[1] * tile_x - 1

    @pl.loop(0, half + 2)
    def _(z):
        z_place = z_base + z + upper * half
        z_valid = jnp.logical_and(z_place >= 0, z_place < tile_z * shot_count)
        for g in range(hidden_x // WIDE):
            window = wide[pl.ds(z, 3), g]
            got = jnp.dot(
                w1[...], window.reshape(-1, lanes), preferred_element_type=jnp.float32
            )
            for i in range(WIDE):
                x = g * WIDE + i
                x_place = x_base + x
                x_valid = jnp.logical_and(x_place >= 0, x_place < tile_x * slab_count)
                valid = jnp.logical_and(z_valid, x_valid)
                value = jnp.maximum(got[i * channels:(i + 1) * channels] + b1, 0.0)
                value = jnp.where(valid, value, 0.0)
                for k, part in enumerate(three(value)):
                    hidden[z, x, k * channels:(k + 1) * channels, :] = part

    chunk = min(16, tile_x)

    @pl.loop(0, half)
    def _(z):
        for c in range(tile_x // chunk):
            parts = []
            for g in range(chunk // OUT):
                x = c * chunk + g * OUT
                window = hidden[pl.ds(z, 3), x:x + OUT + 2]
                got = jnp.dot(
                    w2[...], window.reshape(-1, lanes), preferred_element_type=jnp.float32
                )
                parts.append(jnp.maximum(got + b2, 0.0))
            for h in range(2):
                pieces = [
                    p[:, h * y:(h + 1) * y].reshape(out_channels, OUT, y) for p in parts
                ]
                block = pieces[0] if len(pieces) == 1 else jnp.concatenate(pieces, axis=1)
                out[:, z + h * half, c * chunk:(c + 1) * chunk, :] = block.astype(out.dtype)


def convolutions(
    got, first_weight, first_bias, second_weight, second_bias, tile_z, tile_x, shots_here
):
    shot_count, slab_count = lax.axis_size("shot"), lax.axis_size("slab")
    channels, inputs = first_weight.shape[:2]
    out_channels = second_weight.shape[0]
    y = got.shape[3]
    half = tile_z // 2
    hidden_x = -(-(tile_x + 2) // WIDE) * WIDE
    depth = inputs * (WIDE + 2)
    k1 = 9 * depth
    w1 = jnp.transpose(first_weight, (0, 2, 4, 1, 3))
    w1 = jnp.pad(w1, ((0, 0),) * 4 + ((0, WIDE - 1),)).reshape(channels, k1)
    w1 = jnp.pad(w1, ((0, 0), (0, lanes_for(k1) - k1))).astype(jnp.float32)
    w2 = jnp.transpose(second_weight, (0, 2, 3, 4, 1)).reshape(out_channels, 3, 3, 3 * channels)
    k2 = 3 * (OUT + 2) * 3 * channels
    w2 = spread(w2, OUT, lanes_for(k2))
    b1 = first_bias[None]
    b2 = second_bias[None]
    place = jnp.stack([lax.axis_index("shot"), lax.axis_index("slab")]).astype(jnp.int32)
    vmem = pl.BlockSpec(memory_space=pltpu.VMEM)
    return pl.pallas_call(
        functools.partial(conv_kernel, tile_z, tile_x, shot_count, slab_count, shots_here),
        out_shape=jax.ShapeDtypeStruct((out_channels, tile_z, tile_x, y), jnp.bfloat16),
        in_specs=[pl.BlockSpec(memory_space=pltpu.SMEM)] + [vmem] * 5,
        out_specs=vmem,
        scratch_shapes=[
            pltpu.VMEM((half + 4, hidden_x // WIDE, 3 * depth, 2 * y), jnp.bfloat16),
            pltpu.VMEM((half + 2, hidden_x, 3 * channels, 2 * y), jnp.bfloat16),
            pltpu.VMEM((WIDE * channels, k1), jnp.bfloat16),
            pltpu.VMEM((OUT * out_channels, k2), jnp.bfloat16),
            pltpu.VMEM((2, shot_count) + got.shape[2:], jnp.float32),
        ],
        compiler_params=pltpu.CompilerParams(vmem_limit_bytes=48 * 1024 * 1024),
        name="convolutions",
    )(place, got, w1, b1, w2, b2)


def shards(
    source_field, receiver_field, shot_group, first_weight, first_bias, second_weight, second_bias
):
    shots_here, _, slab_z, all_x, _ = source_field.shape
    shot_count, slab_count = lax.axis_size("shot"), lax.axis_size("slab")
    tile_z = slab_z * slab_count // shot_count
    tile_x = all_x // slab_count
    got = exchange(source_field, receiver_field)
    weight_of_shot = first_weight.at[:, shot_group].get(
        mode="promise_in_bounds", wrap_negative_indices=False
    )
    return convolutions(
        got, weight_of_shot, first_bias, second_weight, second_bias, tile_z, tile_x, shots_here
    )


def solution(mesh):
    placed = (
        P("shot", None, "slab", None, None),
        P("shot", None, "slab", None, None),
        P(),
        P(),
        P(),
        P(),
        P(),
    )
    return jax.shard_map(
        shards, mesh=mesh, in_specs=placed, out_specs=P(None, "shot", "slab", None), check_vma=False
    )
```
